32 devices in a mesh: row: 8 (over z, core), col: 4 (over y, x).
Axes of the slice: x: 2, y: 2, z: 4, core: 2. Of those that a mesh axis runs over, the one named last changes fastest.
Arguments:
- weather: bfloat16 [192, 1024, 1024], P(None, 'row', 'col'), may hold values from -6 to 6
- cotangent: bfloat16 [192, 1024, 1024], P(None, 'row', 'col'), may hold values from -6 to 6
- spectral_in: bfloat16 [2, 2, 96, 96], replicated, may hold values from -0.4375 to 0.4375
- spectral_bias: float32 [2, 2, 96], replicated, may hold values from -3 to 3
- spectral_out: bfloat16 [2, 2, 96, 96], replicated, may hold values from -1.75 to 1.75
- project_in: bfloat16 [192, 768], replicated, may hold values from -0.4375 to 0.4375
- project_out: bfloat16 [768, 192], replicated, may hold values from -0.21875 to 0.21875
Outputs:
- layer_out: bfloat16 [192, 1024, 1024], P(None, 'row', 'col')
- grad_weather: bfloat16 [192, 1024, 1024], P(None, 'row', 'col')
- grad_project_in: float32 [192, 768], replicated
- grad_project_out: float32 [768, 192], replicated
- grad_spectral_in: float32 [2, 2, 96, 96], replicated
- grad_spectral_out: float32 [2, 2, 96, 96], replicated
- grad_spectral_bias: float32 [2, 2, 96], replicated
The draws below stay inside these ranges and needn't reach their ends.
All inputs are finite; a program needn't handle non-finite values.
Results may differ from the reference program's by a relative error of at most 0.019.
The reference program's roundings to bfloat16 on the way count: a program that leaves them out, or rounds other values in their place, can miss the bound.
Values may be sent and summed in bfloat16 or wider, within the bound.
No kernel may reach another device: no remote copies, remote signals or barrier semaphores. Data moves between devices by JAX's collectives and lax.ppermute only.
A program may use at most 512 MiB of HBM per device.

```python
import math
import jax
import jax.numpy as jnp
from jax import lax

H = 1024
W = 1024
NB = 2
BS = 96
C = 192
HID = 768
KH = 512
KW = 256


def level_of(stream_key, extent, split, least, top_value):
    level, own = 1.0, jax.random.fold_in(stream_key, 6)
    for axis_at, parts in split:
        draws = jnp.exp(jax.random.uniform(jax.random.fold_in(own, axis_at), (parts,), jnp.float32, least / len(split), top_value / len(split)))
        level = level * jnp.repeat(draws, extent[axis_at] // parts).reshape([-1 if axis == axis_at else 1 for axis in range(len(extent))])
    return level


def scatter_about(stream_key, dims, scale, reach, cuts=(), kind=jnp.bfloat16):
    factor_of = level_of(stream_key, dims, cuts, -0.22, 0.18) if cuts else 1.0
    values = jax.random.normal(stream_key, dims, jnp.float32) * scale * factor_of
    return jnp.minimum(jnp.maximum(values, -reach), reach).astype(kind)


def setup_inputs(seed: int = 0) -> dict:
    key_list = jax.random.split(jax.random.key(seed), 8)
    return {
        "weather": scatter_about(key_list[0], (C, H, W), 1.0, 6.0, ((1, 8), (2, 4))),
        "cotangent": scatter_about(key_list[1], (C, H, W), 1.0, 6.0, ((1, 8), (2, 4))),
        "spectral_in": scatter_about(key_list[2], (2, NB, BS, BS), (2 * BS) ** -0.5, 0.4375),
        "spectral_bias": scatter_about(key_list[3], (2, NB, BS), 0.5, 3.0, (), jnp.float32),
        "spectral_out": scatter_about(key_list[4], (2, NB, BS, BS), (BS // 8) ** -0.5, 1.75),
        "project_in": scatter_about(key_list[5], (C, HID), C ** -0.5, 0.4375),
        "project_out": scatter_about(key_list[6], (HID, C), HID ** -0.5, 0.21875),
    }


epsilon = 1e-05
threshold = 0.1

def product(form, left, right):
    return jnp.einsum(form, left.astype(jnp.float32), right.astype(jnp.float32))

def gelu_slope(values):
    return 0.5 * (1.0 + lax.erf(values * (1.0 / math.sqrt(2.0)))) + values * jnp.exp(-0.5 * values * values) * (1.0 / math.sqrt(2.0 * math.pi))

def width_tables(width, kept):
    position = jnp.arange(width, dtype=jnp.int32)
    frequency = jnp.arange(kept, dtype=jnp.int32)
    phases = position[:, None] * frequency[None, :] % width
    angles = phases.astype(jnp.float32) * (2.0 * math.pi / width)
    factor = 1.0 / math.sqrt(width)
    weight = jnp.where(frequency == 0, 1.0, 2.0).astype(jnp.float32)
    cosine = jnp.cos(angles) * factor
    sine_values = -jnp.sin(angles) * factor
    return (cosine.astype(jnp.bfloat16), sine_values.astype(jnp.bfloat16), (cosine * weight[None, :]).astype(jnp.bfloat16), (sine_values * weight[None, :]).astype(jnp.bfloat16))

def height_tables(height, kept):
    position = jnp.arange(height, dtype=jnp.int32)
    indices = jnp.arange(kept, dtype=jnp.int32)
    frequency = jnp.where(indices < kept // 2, indices, indices + (height - kept))
    phases = position[:, None] * frequency[None, :] % height
    angles = phases.astype(jnp.float32) * (2.0 * math.pi / height)
    factor = 1.0 / math.sqrt(height)
    return ((jnp.cos(angles) * factor).astype(jnp.bfloat16), (-jnp.sin(angles) * factor).astype(jnp.bfloat16))

def width_forward(field_part, cosine_table, sine_table):
    real_part = product('crw,wk->rkc', field_part, cosine_table)
    imaginary = product('crw,wk->rkc', field_part, sine_table)
    return jnp.stack([real_part, imaginary], axis=2).astype(jnp.bfloat16)

def width_inverse(spectrum, cosine_table, sine_table):
    half_width = spectrum.shape[2] // 2
    summed = product('rkc,wk->crw', spectrum[:, :, :half_width], cosine_table)
    summed = summed + product('rkc,wk->crw', spectrum[:, :, half_width:], sine_table)
    return summed.astype(jnp.bfloat16)

def height_forward(spectrum, real_table, imaginary_table):
    half_width = spectrum.shape[2] // 2
    first_term = product('hnx,hm->mnx', spectrum, real_table)
    second = product('hnx,hm->mnx', spectrum, imaginary_table)
    return jnp.concatenate([first_term[:, :, :half_width] - second[:, :, half_width:], first_term[:, :, half_width:] + second[:, :, :half_width]], axis=2)

def height_inverse(kept_modes, real_table, imaginary_table):
    half_width = kept_modes.shape[2] // 2
    first_term = product('mnx,hm->hnx', kept_modes, real_table)
    second = product('mnx,hm->hnx', kept_modes, imaginary_table)
    return jnp.concatenate([first_term[:, :, :half_width] + second[:, :, half_width:], first_term[:, :, half_width:] - second[:, :, :half_width]], axis=2)

def soft_shrink(values):
    return values - threshold * jnp.tanh(values * (1.0 / threshold))

def shrink_slope(values):
    return jnp.square(jnp.tanh(values * (1.0 / threshold)))

def spectral_forward(kept_modes, spectral_in, spectral_bias, spectral_out):
    mode_count, column_count, doubled = kept_modes.shape
    pieces = kept_modes.reshape(mode_count, column_count, 2, NB, BS)
    real_input, imaginary_input = (pieces[:, :, 0], pieces[:, :, 1])
    before_real = product('mnbi,bio->mnbo', real_input, spectral_in[0]) - product('mnbi,bio->mnbo', imaginary_input, spectral_in[1]) + spectral_bias[0]
    before_imaginary = product('mnbi,bio->mnbo', imaginary_input, spectral_in[0]) + product('mnbi,bio->mnbo', real_input, spectral_in[1]) + spectral_bias[1]
    hidden_real = jax.nn.gelu(before_real, approximate=False).astype(jnp.bfloat16)
    hidden_imaginary = jax.nn.gelu(before_imaginary, approximate=False).astype(jnp.bfloat16)
    second_real = product('mnbi,bio->mnbo', hidden_real, spectral_out[0]) - product('mnbi,bio->mnbo', hidden_imaginary, spectral_out[1])
    second_imaginary = product('mnbi,bio->mnbo', hidden_imaginary, spectral_out[0]) + product('mnbi,bio->mnbo', hidden_real, spectral_out[1])
    shrunk = jnp.stack([soft_shrink(second_real), soft_shrink(second_imaginary)], axis=2)
    shrunk = shrunk.reshape(mode_count, column_count, doubled).astype(jnp.bfloat16)
    return (shrunk, (before_real, before_imaginary, hidden_real, hidden_imaginary, second_real, second_imaginary))

def spectral_backward(gradient, kept_modes, saved, spectral_in, spectral_out):
    mode_count, column_count, doubled = gradient.shape
    grad_pieces = gradient.reshape(mode_count, column_count, 2, NB, BS)
    pieces = kept_modes.reshape(mode_count, column_count, 2, NB, BS)
    real_input, imaginary_input = (pieces[:, :, 0], pieces[:, :, 1])
    before_real, before_imaginary, hidden_real, hidden_imaginary, second_real, second_imaginary = saved
    keep_real = (grad_pieces[:, :, 0] * shrink_slope(second_real)).astype(jnp.bfloat16)
    keep_imaginary = (grad_pieces[:, :, 1] * shrink_slope(second_imaginary)).astype(jnp.bfloat16)
    back_real = product('mnbo,bio->mnbi', keep_real, spectral_out[0]) + product('mnbo,bio->mnbi', keep_imaginary, spectral_out[1])
    back_imaginary = product('mnbo,bio->mnbi', keep_imaginary, spectral_out[0]) - product('mnbo,bio->mnbi', keep_real, spectral_out[1])
    out_real = product('mnbi,mnbo->bio', hidden_real, keep_real) + product('mnbi,mnbo->bio', hidden_imaginary, keep_imaginary)
    out_imaginary = product('mnbi,mnbo->bio', hidden_real, keep_imaginary) - product('mnbi,mnbo->bio', hidden_imaginary, keep_real)
    gate_real = (back_real * gelu_slope(before_real)).astype(jnp.bfloat16)
    gate_imaginary = (back_imaginary * gelu_slope(before_imaginary)).astype(jnp.bfloat16)
    in_real = product('mnbi,mnbo->bio', real_input, gate_real) + product('mnbi,mnbo->bio', imaginary_input, gate_imaginary)
    in_imaginary = product('mnbi,mnbo->bio', real_input, gate_imaginary) - product('mnbi,mnbo->bio', imaginary_input, gate_real)
    bias_grad = jnp.stack([lax.optimization_barrier(jnp.sum(gate_real.astype(jnp.float32), axis=(0, 1))), lax.optimization_barrier(jnp.sum(gate_imaginary.astype(jnp.float32), axis=(0, 1)))])
    input_real = product('mnbo,bio->mnbi', gate_real, spectral_in[0]) + product('mnbo,bio->mnbi', gate_imaginary, spectral_in[1])
    input_imaginary = product('mnbo,bio->mnbi', gate_imaginary, spectral_in[0]) - product('mnbo,bio->mnbi', gate_real, spectral_in[1])
    grad_modes = jnp.stack([input_real, input_imaginary], axis=2)
    grad_modes = grad_modes.reshape(mode_count, column_count, doubled).astype(jnp.bfloat16)
    return (grad_modes, jnp.stack([in_real, in_imaginary]), jnp.stack([out_real, out_imaginary]), bias_grad)

def layer_norm(flat_field):
    centred = flat_field - lax.optimization_barrier(jnp.mean(flat_field, axis=0, keepdims=True))
    variance = lax.optimization_barrier(jnp.mean(centred * centred, axis=0, keepdims=True))
    inverse_spread = lax.rsqrt(variance + epsilon)
    return (centred * inverse_spread, inverse_spread)

def norm_backward(normed, inverse_spread, gradient):
    mean_grad = lax.optimization_barrier(jnp.mean(gradient, axis=0, keepdims=True))
    mean_cross = lax.optimization_barrier(jnp.mean(gradient * normed, axis=0, keepdims=True))
    return inverse_spread * (gradient - mean_grad - normed * mean_cross)

def token_block(weather, normed_in, filtered, cotangent, project_in, project_out):
    channels = weather.shape[0]
    summed = weather.astype(jnp.float32) + normed_in.astype(jnp.float32) + filtered.astype(jnp.float32)
    flat_sum = summed.reshape(channels, -1)
    normed, inverse_spread = layer_norm(flat_sum)
    normed_low = normed.astype(jnp.bfloat16)
    before = product('cn,ch->hn', normed_low, project_in)
    hidden = jax.nn.gelu(before, approximate=False).astype(jnp.bfloat16)
    output = (flat_sum + product('hn,hc->cn', hidden, project_out)).astype(jnp.bfloat16)
    flat_cot = cotangent.reshape(channels, -1)
    back_hidden = product('cn,hc->hn', flat_cot, project_out)
    back_before = (back_hidden * gelu_slope(before)).astype(jnp.bfloat16)
    grad_out = product('hn,cn->hc', hidden, flat_cot)
    grad_in = product('cn,hn->ch', normed_low, back_before)
    back_normed = product('hn,ch->cn', back_before, project_in)
    grad_sum = flat_cot.astype(jnp.float32) + norm_backward(normed, inverse_spread, back_normed)
    return (output.reshape(weather.shape), grad_sum.reshape(weather.shape), grad_in, grad_out)

def reference(weather, cotangent, spectral_in, spectral_bias, spectral_out, project_in, project_out):
    cosine, sine_table, cosine_weighted, sine_weighted = width_tables(W, KW)
    real_table, imaginary_table = height_tables(H, KH)
    block_count = 16
    block_rows = H // block_count

    def to_blocks(field_whole):
        return field_whole.reshape(C, block_count, block_rows, W).transpose(1, 0, 2, 3)

    def from_blocks(field_blocks):
        return field_blocks.transpose(1, 0, 2, 3).reshape(C, H, W)
    weather_blocks = to_blocks(weather)
    cot_blocks = to_blocks(cotangent)

    def section_one(row_block):
        normed, inverse_spread = layer_norm(row_block.astype(jnp.float32).reshape(C, -1))
        normed_low = normed.astype(jnp.bfloat16).reshape(row_block.shape)
        spectrum = width_forward(normed_low, cosine, sine_table).reshape(block_rows, KW, 2 * C)
        return (normed_low, spectrum)
    normed_blocks, spectrum = lax.map(section_one, weather_blocks)
    kept_low = height_forward(spectrum.reshape(H, KW, 2 * C), real_table, imaginary_table).astype(jnp.bfloat16)
    shrunk, saved = spectral_forward(kept_low, spectral_in, spectral_bias, spectral_out)
    back = height_inverse(shrunk, real_table, imaginary_table).astype(jnp.bfloat16)
    back = back.reshape(block_count, block_rows, KW, 2 * C)

    def section_two(pieces):
        row_block, normed_low, back_block, cot_block = pieces
        filtered = width_inverse(back_block, cosine_weighted, sine_weighted)
        output, grad_sum, grad_in, grad_out = token_block(row_block, normed_low, filtered, cot_block, project_in, project_out)
        grad_spectrum = width_forward(grad_sum.astype(jnp.bfloat16), cosine_weighted, sine_weighted)
        return (output, grad_sum, grad_spectrum.reshape(block_rows, KW, 2 * C), grad_in, grad_out)
    output, grad_sum, grad_spectrum, grad_in, grad_out = lax.map(section_two, (weather_blocks, normed_blocks, back, cot_blocks))
    grad_kept = height_forward(grad_spectrum.reshape(H, KW, 2 * C), real_table, imaginary_table)
    grad_modes, grad_first, grad_second, grad_bias = spectral_backward(grad_kept, kept_low, saved, spectral_in, spectral_out)
    grad_back = height_inverse(grad_modes, real_table, imaginary_table).astype(jnp.bfloat16)
    grad_back = grad_back.reshape(block_count, block_rows, KW, 2 * C)

    def section_three(pieces):
        row_block, grad_block, grad_back_block = pieces
        normed, inverse_spread = layer_norm(row_block.astype(jnp.float32).reshape(C, -1))
        grad_normed = grad_block + width_inverse(grad_back_block, cosine, sine_table).astype(jnp.float32)
        result = grad_block.reshape(C, -1) + norm_backward(normed, inverse_spread, grad_normed.reshape(C, -1))
        return result.reshape(row_block.shape).astype(jnp.bfloat16)
    grad_weather = lax.map(section_three, (weather_blocks, grad_sum, grad_back))
    return (from_blocks(output), from_blocks(grad_weather), lax.optimization_barrier(jnp.sum(grad_in, axis=0)) / H, lax.optimization_barrier(jnp.sum(grad_out, axis=0)) / H, grad_first / H, grad_second / H, grad_bias / H)
```

```python
import functools
import math

import jax
import jax.numpy as jnp
import ml_dtypes
import numpy as np
from jax import lax
from jax.experimental import pallas as pl
from jax.experimental.pallas import tpu as pltpu
from jax.sharding import PartitionSpec as P

KH = 512
KW = 256

epsilon = 1e-05
threshold = 0.1
BF16 = jnp.bfloat16
F32 = jnp.float32
EVERY = ("row", "col")
VMEM_BYTES = 56 * 2**20
CHUNK_ROWS = 8
FIRST_US = 60
TOKEN_US = 100
LAST_US = 60
MODES_US = 60
RELAYOUT_US = 12


def width_tables(width, kept):
    position = np.arange(width, dtype=np.int32)
    frequency = np.arange(kept, dtype=np.int32)
    phases = position[:, None] * frequency[None, :] % width
    angles = phases.astype(np.float32) * np.float32(2.0 * math.pi / width)
    factor = np.float32(1.0 / math.sqrt(width))
    weight = np.where(frequency == 0, 1.0, 2.0).astype(np.float32)
    cosine = np.cos(angles) * factor
    sine_values = -np.sin(angles) * factor
    plain = np.concatenate([cosine, sine_values], axis=1)
    weighted = np.concatenate([cosine * weight[None, :], sine_values * weight[None, :]], axis=1)
    return plain.astype(ml_dtypes.bfloat16), weighted.astype(ml_dtypes.bfloat16)


def height_tables(height, kept):
    position = np.arange(height, dtype=np.int32)
    indices = np.arange(kept, dtype=np.int32)
    frequency = np.where(indices < kept // 2, indices, indices + (height - kept))
    phases = position[:, None] * frequency[None, :] % height
    angles = phases.astype(np.float32) * np.float32(2.0 * math.pi / height)
    factor = np.float32(1.0 / math.sqrt(height))
    both = np.concatenate([np.cos(angles) * factor, -np.sin(angles) * factor], axis=1)
    return both.astype(ml_dtypes.bfloat16)


def dot(left, right):
    return jnp.dot(left, right, preferred_element_type=F32)


def dot_rows(left, right):
    return lax.dot_general(left, right, (((1,), (1,)), ((), ())), preferred_element_type=F32)


def dot_columns(left, right):
    return lax.dot_general(left, right, (((0,), (0,)), ((), ())), preferred_element_type=F32)


def gelu_parts(values):
    share = 0.5 * (1.0 + lax.erf(values * (1.0 / math.sqrt(2.0))))
    density = jnp.exp(-0.5 * values * values) * (1.0 / math.sqrt(2.0 * math.pi))
    return share, share + values * density


def layer_norm(field):
    centred = field - jnp.mean(field, axis=0, keepdims=True)
    variance = jnp.mean(centred * centred, axis=0, keepdims=True)
    inverse_spread = lax.rsqrt(variance + epsilon)
    return centred * inverse_spread, inverse_spread


def norm_backward(normed, inverse_spread, gradient):
    mean_grad = jnp.mean(gradient, axis=0, keepdims=True)
    mean_cross = jnp.mean(gradient * normed, axis=0, keepdims=True)
    return inverse_spread * (gradient - mean_grad - normed * mean_cross)


def modes_first(spectrum):
    parts = jnp.concatenate([spectrum[:, :KW], spectrum[:, KW:]], axis=0)
    return parts.T.astype(BF16)


def channels_first(modes):
    turned = modes.astype(F32).T.astype(BF16)
    half = turned.shape[0] // 2
    return jnp.concatenate([turned[:half], turned[half:]], axis=1)


def first_kernel(count, order, *refs):
    fields, table, out = refs[:count], refs[count], refs[count + 1]
    total = None
    for slot in range(count):
        normed, _ = layer_norm(fields[slot][0].astype(F32))
        part = dot(normed.astype(BF16), table[order[slot]])
        total = part if total is None else total + part
    out[0] = modes_first(total)


def token_kernel(count, order, *refs):
    fields, cotangents = refs[:count], refs[count : 2 * count]
    back, inverse, forward, into, into_turned, onto, onto_turned = refs[2 * count : 2 * count + 7]
    outs = refs[2 * count + 7 : 3 * count + 7]
    kept_sum, spectrum, grad_onto, grad_into = refs[3 * count + 7 :]

    @pl.when(pl.program_id(0) == 0)
    def _():
        grad_onto[...] = jnp.zeros_like(grad_onto)
        grad_into[...] = jnp.zeros_like(grad_into)

    modes = channels_first(back[0])
    total = None
    for slot in range(count):
        field = fields[slot][0].astype(F32)
        normed_in = layer_norm(field)[0].astype(BF16)
        filtered = dot(modes, inverse[order[slot]]).astype(BF16)
        summed = field + normed_in.astype(F32) + filtered.astype(F32)
        normed, inverse_spread = layer_norm(summed)
        normed_low = normed.astype(BF16)
        cotangent = cotangents[slot][0]
        before = dot(into_turned[...], normed_low)
        back_hidden = dot(onto[...], cotangent)
        share, slope = gelu_parts(before)
        hidden = (before * share).astype(BF16)
        back_before = (back_hidden * slope).astype(BF16)
        outs[slot][0] = (summed + dot(onto_turned[...], hidden)).astype(BF16)
        grad_onto[...] += dot_rows(hidden, cotangent)
        grad_into[...] += dot_rows(back_before, normed_low)
        back_normed = dot(into[...], back_before)
        grad_sum = cotangent.astype(F32) + norm_backward(normed, inverse_spread, back_normed)
        kept_sum[0, slot] = grad_sum
        part = dot(grad_sum.astype(BF16), forward[order[slot]])
        total = part if total is None else total + part
    spectrum[0] = modes_first(total)


def last_kernel(count, order, *refs):
    fields, kept_sum, back, inverse = refs[:count], refs[count], refs[count + 1], refs[count + 2]
    outs = refs[count + 3 :]
    modes = channels_first(back[0])
    for slot in range(count):
        normed, inverse_spread = layer_norm(fields[slot][0].astype(F32))
        filtered = dot(modes, inverse[order[slot]]).astype(BF16)
        grad_sum = kept_sum[0, slot]
        grad_normed = grad_sum + filtered.astype(F32)
        outs[slot][0] = (grad_sum + norm_backward(normed, inverse_spread, grad_normed)).astype(BF16)


def swap_parts(values):
    lane = lax.broadcasted_iota(jnp.int32, values.shape, 1)
    half = values.shape[1] // 2
    turned = pltpu.roll(values, half, 1)
    return jnp.where(lane < half, -turned, turned)


def to_kept(pieces, table):
    rows = jnp.concatenate([piece[0] for piece in pieces], axis=0) if len(pieces) > 1 else pieces[0][0]
    both = dot(table[...], rows)
    return both[:KH] + swap_parts(both[KH:])


def from_kept(modes, table, outs):
    both = jnp.concatenate([modes.astype(BF16), (-swap_parts(modes)).astype(BF16)], axis=0)
    rows = dot(table[...], both).astype(BF16)
    size = rows.shape[0] // len(outs)
    for at, out in enumerate(outs):
        out[0] = rows[at * size : (at + 1) * size]


def modes_kernel(count, *refs):
    pieces = refs[:count]
    forward, inverse, weight_in, bias, weight_out = refs[count : count + 5]
    outs = refs[count + 5 : 2 * count + 5]
    kept_out, hidden_out, slope_out, shrink_out = refs[2 * count + 5 :]
    kept_low = to_kept(pieces, forward).astype(BF16)
    kept_out[0] = kept_low
    before = dot(kept_low, weight_in[...]) + bias[...]
    share, slope = gelu_parts(before)
    hidden = (before * share).astype(BF16)
    hidden_out[0] = hidden
    slope_out[0] = slope
    second = dot(hidden, weight_out[...])
    level = jnp.tanh(second * (1.0 / threshold))
    shrink_out[0] = level * level
    shrunk = second - threshold * level
    from_kept(shrunk, inverse, outs)


def modes_back_kernel(count, *refs):
    pieces = refs[:count]
    kept, hidden, slope, shrink = refs[count : count + 4]
    forward, inverse, weight_in, weight_out = refs[count + 4 : count + 8]
    outs = refs[count + 8 : 2 * count + 8]
    grad_in, grad_out, grad_bias = refs[2 * count + 8 :]

    @pl.when(pl.program_id(0) == 0)
    def _():
        grad_in[...] = jnp.zeros_like(grad_in)
        grad_out[...] = jnp.zeros_like(grad_out)
        grad_bias[...] = jnp.zeros_like(grad_bias)

    grad_second = (to_kept(pieces, forward) * shrink[0]).astype(BF16)
    grad_out[...] += dot_columns(hidden[0], grad_second)
    back_spec = dot_rows(grad_second, weight_out[...])
    gate = (back_spec * slope[0]).astype(BF16)
    grad_in[...] += dot_columns(kept[0], gate)
    grad_bias[...] += jnp.sum(gate.astype(F32), axis=0, keepdims=True)
    grad_modes = dot_rows(gate, weight_in[...])
    from_kept(grad_modes, inverse, outs)


def whole(array_shape):
    return pl.BlockSpec(array_shape, lambda *at: (0,) * len(array_shape))


def by_first(array_shape):
    rest = len(array_shape) - 1
    return pl.BlockSpec((1,) + tuple(array_shape[1:]), lambda at, *_: (at,) + (0,) * rest)


def params():
    return pltpu.CompilerParams(
        dimension_semantics=("arbitrary",), vmem_limit_bytes=VMEM_BYTES
    )


def weigh(microseconds):
    return pl.CostEstimate(
        flops=int(microseconds * 1.15e9), bytes_accessed=int(microseconds * 3.6e6), transcendentals=0
    )


def leave_out(kernel, start, count):
    def run(*refs):
        kernel(*refs[:start], *refs[start + count :])

    return run


def call_rows(kernel, weight, steps, order, stepped, fixed, step_outs, fixed_outs, waited=()):
    outs = list(step_outs) + list(fixed_outs)
    return pl.pallas_call(
        leave_out(kernel, 1 + len(stepped) + len(fixed), len(waited)),
        grid_spec=pltpu.PrefetchScalarGridSpec(
            num_scalar_prefetch=1,
            grid=(steps,),
            in_specs=[by_first(a.shape) for a in stepped]
            + [whole(a.shape) for a in fixed]
            + [pl.BlockSpec(memory_space=pl.ANY)] * len(waited),
            out_specs=[by_first(a.shape) for a in step_outs] + [whole(a.shape) for a in fixed_outs],
        ),
        out_shape=outs,
        compiler_params=params(),
        cost_estimate=weigh(weight),
    )(order, *stepped, *fixed, *waited)


def call_modes(kernel, weight, steps, stepped, fixed, step_outs, fixed_outs, waited=()):
    outs = list(step_outs) + list(fixed_outs)
    return pl.pallas_call(
        leave_out(kernel, len(stepped) + len(fixed), len(waited)),
        grid=(steps,),
        in_specs=[by_first(a.shape) for a in stepped]
        + [whole(a.shape) for a in fixed]
        + [pl.BlockSpec(memory_space=pl.ANY)] * len(waited),
        out_specs=[by_first(a.shape) for a in step_outs] + [whole(a.shape) for a in fixed_outs],
        out_shape=outs,
        compiler_params=params(),
        cost_estimate=weigh(weight),
    )(*stepped, *fixed, *waited)


def split_kernel(order, field, *outs):
    rows = jnp.swapaxes(field[:, 0], 0, 1)
    size = rows.shape[0] // len(outs)
    for at, out in enumerate(outs):
        out[0] = rows[at * size : (at + 1) * size]


def split_rows(field, order, own_rows, first, chunk, count):
    channels, local_rows, local_cols = field.shape
    groups, size = local_rows // own_rows, count * chunk
    return pl.pallas_call(
        split_kernel,
        grid_spec=pltpu.PrefetchScalarGridSpec(
            num_scalar_prefetch=1,
            grid=(groups,),
            in_specs=[
                pl.BlockSpec(
                    (channels, 1, size, local_cols), lambda at, order: (0, order[at], first // size, 0)
                )
            ],
            out_specs=[
                pl.BlockSpec((1, chunk, channels, local_cols), lambda at, order: (at, 0, 0, 0))
            ]
            * count,
        ),
        out_shape=[jax.ShapeDtypeStruct((groups, chunk, channels, local_cols), BF16)] * count,
        compiler_params=params(),
        cost_estimate=weigh(RELAYOUT_US),
    )(order, field.reshape(channels, groups, own_rows, local_cols))


def join_kernel(groups, count, order, *refs):
    pieces, out = refs[: groups * count], refs[-1]
    for slot in range(groups):

        @pl.when(pl.program_id(0) == slot)
        def _():
            rows = [pieces[at * groups + slot][...] for at in range(count)]
            out[...] = jnp.swapaxes(jnp.concatenate(rows, axis=0), 0, 1)


def join_rows(total, order, own_rows, first, per_chunk):
    groups, count = len(per_chunk[0]), len(per_chunk)
    chunk, channels, local_cols = per_chunk[0][0].shape
    size = count * chunk
    pieces = [piece for chunk_pieces in per_chunk for piece in chunk_pieces]
    given = [] if total is None else [total]
    return pl.pallas_call(
        functools.partial(join_kernel, groups, count),
        grid_spec=pltpu.PrefetchScalarGridSpec(
            num_scalar_prefetch=1,
            grid=(groups,),
            in_specs=[pl.BlockSpec(piece.shape, lambda at, order: (0, 0, 0)) for piece in pieces]
            + [pl.BlockSpec(memory_space=pl.ANY)] * len(given),
            out_specs=pl.BlockSpec(
                (channels, size, local_cols),
                lambda at, order: (0, order[at] * (own_rows // size) + first // size, 0),
            ),
        ),
        out_shape=jax.ShapeDtypeStruct((channels, groups * own_rows, local_cols), BF16),
        input_output_aliases={1 + len(pieces): 0} if given else {},
        compiler_params=params(),
        cost_estimate=weigh(RELAYOUT_US),
    )(order, *pieces, *given)


def scale_kernel(factor, *refs):
    count = len(refs) // 2
    for source, out in zip(refs[:count], refs[count:]):
        out[...] = source[...] * factor


def scale(arrays, factor, waited):
    return pl.pallas_call(
        leave_out(functools.partial(scale_kernel, factor), len(arrays), len(waited)),
        in_specs=[pl.BlockSpec(memory_space=pltpu.VMEM)] * len(arrays)
        + [pl.BlockSpec(memory_space=pl.ANY)] * len(waited),
        out_specs=[pl.BlockSpec(memory_space=pltpu.VMEM)] * len(arrays),
        out_shape=[jax.ShapeDtypeStruct(a.shape, a.dtype) for a in arrays],
        compiler_params=pltpu.CompilerParams(vmem_limit_bytes=VMEM_BYTES),
    )(*arrays, *waited)


def complex_matrix(weight):
    blocks, size = weight.shape[1], weight.shape[2]

    def diagonal(part):
        rows = []
        for at in range(blocks):
            rows.append(jnp.pad(part[at], ((0, 0), (at * size, (blocks - 1 - at) * size))))
        return jnp.concatenate(rows, axis=0)

    real, imaginary = diagonal(weight[0]), diagonal(weight[1])
    return jnp.concatenate(
        [
            jnp.concatenate([real, imaginary], axis=1),
            jnp.concatenate([-imaginary, real], axis=1),
        ],
        axis=0,
    )


def complex_gradient(total, blocks):
    half = total.shape[0] // 2
    size = half // blocks
    real = total[:half, :half] + total[half:, half:]
    imaginary = total[:half, half:] - total[half:, :half]

    def blocked(part):
        return jnp.stack(
            [
                part[at * size : (at + 1) * size, at * size : (at + 1) * size]
                for at in range(blocks)
            ]
        )

    return jnp.stack([blocked(real), blocked(imaginary)])


def body(
    row_count,
    col_count,
    weather,
    cotangent,
    spectral_in,
    spectral_bias,
    spectral_out,
    project_in,
    project_out,
):
    channels, local_rows, local_cols = weather.shape
    height, width = local_rows * row_count, local_cols * col_count
    devices = row_count * col_count
    own_rows = local_rows // col_count
    chunk = min(CHUNK_ROWS, own_rows)
    chunks = own_rows // chunk
    own_modes = KW // devices
    doubled = 2 * channels
    hidden_units = project_in.shape[1]
    blocks = spectral_in.shape[1]

    paired = col_count & (col_count - 1) == 0
    column = lax.axis_index("col")
    slots = jnp.arange(col_count, dtype=jnp.int32)
    target = column ^ slots if paired else (column + slots) % col_count
    origin = column ^ slots if paired else (column - slots) % col_count

    def partner(at, slot):
        return at ^ slot if paired else (at + slot) % col_count

    def send(piece, slot):
        if slot == 0:
            return piece
        return lax.ppermute(piece, "col", [(at, partner(at, slot)) for at in range(col_count)])

    def send_back(piece, slot):
        if slot == 0:
            return piece
        return lax.ppermute(piece, "col", [(partner(at, slot), at) for at in range(col_count)])

    def exchange(spectrum):
        return lax.all_to_all(spectrum, EVERY, split_axis=0, concat_axis=0, tiled=True)

    plain, weighted = width_tables(width, KW)
    forward_plain = jnp.asarray(plain.reshape(col_count, local_cols, 2 * KW))
    forward_weighted = jnp.asarray(weighted.reshape(col_count, local_cols, 2 * KW))
    inverse_plain = jnp.asarray(
        np.ascontiguousarray(plain.reshape(col_count, local_cols, 2 * KW).transpose(0, 2, 1))
    )
    inverse_weighted = jnp.asarray(
        np.ascontiguousarray(weighted.reshape(col_count, local_cols, 2 * KW).transpose(0, 2, 1))
    )
    row_order = np.arange(height).reshape(devices, chunks, chunk).transpose(1, 0, 2).reshape(-1)
    by_rows = height_tables(height, KH)[row_order]
    modes_inverse = jnp.asarray(by_rows)
    modes_forward = jnp.asarray(np.ascontiguousarray(by_rows.T))

    matrix_in, matrix_out = complex_matrix(spectral_in), complex_matrix(spectral_out)
    bias_row = spectral_bias.reshape(1, doubled)
    into_turned, onto_turned = project_in.T, project_out.T

    pair = 2 if chunks % 2 == 0 else 1

    def field_pieces(field, at):
        split = split_rows(field, target, own_rows, at * chunk, chunk, pair)
        return [[send(rows[slot], slot) for slot in range(col_count)] for rows in split]

    def to_modes(spectrum):
        parted = spectrum.reshape(chunk, devices, own_modes, doubled).transpose(1, 0, 2, 3)
        got = exchange(parted.reshape(devices, chunk * own_modes, doubled))
        got = got.reshape(devices * chunk, own_modes, doubled)
        return got.transpose(1, 0, 2)

    def to_rows(modes):
        parted = modes.reshape(own_modes, devices, chunk, doubled).transpose(1, 2, 0, 3)
        got = exchange(parted.reshape(devices, chunk * own_modes, doubled))
        got = got.reshape(devices, chunk, own_modes, doubled).transpose(1, 0, 2, 3)
        return got.reshape(chunk, KW, doubled)

    def place(total, pieces, at):
        for slot in range(col_count):
            total = lax.dynamic_update_slice(
                total, pieces[slot].transpose(1, 0, 2), (0, target[slot] * own_rows + at * chunk, 0)
            )
        return total

    def shape(*dims, kind=BF16):
        return jax.ShapeDtypeStruct(dims, kind)

    piece_shape = shape(chunk, channels, local_cols)
    spectrum_shape = shape(chunk, KW, doubled)
    rows_shape = shape(own_modes, devices * chunk, doubled)

    weather_now = sum([field_pieces(weather, at) for at in range(0, chunks, pair)], [])
    cot_now = sum([field_pieces(cotangent, at) for at in range(0, chunks, pair)], [])
    spectra = []
    for at in range(chunks):
        (spectrum,) = call_rows(
            functools.partial(first_kernel, col_count),
            FIRST_US,
            chunk,
            origin,
            weather_now[at],
            [forward_plain],
            [spectrum_shape],
            [],
        )
        spectra.append(to_modes(spectrum))

    mode_dims = (own_modes, KH, doubled)
    results = call_modes(
        functools.partial(modes_kernel, chunks),
            MODES_US,
        own_modes,
        spectra,
        [modes_forward, modes_inverse, matrix_in, bias_row, matrix_out],
        [rows_shape] * chunks
        + [shape(*mode_dims), shape(*mode_dims), shape(*mode_dims, kind=F32), shape(*mode_dims, kind=F32)],
        [],
        waited=[piece for pieces in cot_now[: chunks // 2] for piece in pieces],
    )
    back, saved = results[:chunks], results[chunks:]

    outputs, kept_sums, grad_spectra, grad_onto, grad_into = [], [], [], 0.0, 0.0
    for at in range(chunks):
        results = call_rows(
            functools.partial(token_kernel, col_count),
            TOKEN_US,
            chunk,
            origin,
            weather_now[at] + cot_now[at] + [to_rows(back[at])],
            [
                inverse_weighted,
                forward_weighted,
                project_in,
                into_turned,
                project_out,
                onto_turned,
            ],
            [piece_shape] * col_count
            + [shape(chunk, col_count, channels, local_cols, kind=F32), spectrum_shape],
            [shape(hidden_units, channels, kind=F32)] * 2,
        )
        spectrum = results[col_count + 1]
        outputs.append([send_back(results[slot], slot) for slot in range(col_count)])
        kept_sums.append(results[col_count])
        grad_spectra.append(to_modes(spectrum))
        grad_onto = grad_onto + results[col_count + 2]
        grad_into = grad_into + results[col_count + 3]
    early = chunks // 2
    results = call_modes(
        functools.partial(modes_back_kernel, chunks),
            MODES_US,
        own_modes,
        grad_spectra + list(saved),
        [modes_forward, modes_inverse, matrix_in, matrix_out],
        [rows_shape] * chunks,
        [
            shape(doubled, doubled, kind=F32),
            shape(doubled, doubled, kind=F32),
            shape(1, doubled, kind=F32),
        ],
        waited=[piece for pieces in outputs[:early] for piece in pieces],
    )
    grad_back = results[:chunks]
    grad_in_total, grad_out_total, grad_bias_total = results[chunks:]

    spectral_grads = jnp.stack(
        [complex_gradient(grad_in_total, blocks), complex_gradient(grad_out_total, blocks)]
    )
    packed = jnp.concatenate([spectral_grads.reshape(-1), grad_bias_total.reshape(-1)])
    token_grads, packed = lax.psum(
        (jnp.concatenate([grad_onto, grad_into], axis=0), packed.reshape(-1, 128)), EVERY
    )

    grads = []
    for at in range(chunks):
        results = call_rows(
            functools.partial(last_kernel, col_count),
            LAST_US,
            chunk,
            origin,
            weather_now[at] + [kept_sums[at], to_rows(grad_back[at])],
            [inverse_plain],
            [piece_shape] * col_count,
            [],
            waited=outputs[early + at // 2] if at % 2 == 0 and early + at // 2 < chunks else [],
        )
        grads.append([send_back(results[slot], slot) for slot in range(col_count)])
    token_grads, packed = scale([token_grads, packed], 1.0 / height, [results[0]])

    layer_out = None
    for at in range(0, chunks, pair):
        layer_out = join_rows(layer_out, target, own_rows, at * chunk, outputs[at : at + pair])
    grad_weather = join_rows(None, target, own_rows, 0, grads[:pair])
    for at in range(pair, chunks):
        grad_weather = place(grad_weather, grads[at], at)
    packed = packed.reshape(-1)
    spectral_grads = packed[:-doubled].reshape(spectral_grads.shape)
    return (
        layer_out,
        grad_weather,
        token_grads[hidden_units:].T,
        token_grads[:hidden_units],
        spectral_grads[0],
        spectral_grads[1],
        packed[-doubled:].reshape(spectral_bias.shape),
    )


def solution(mesh):
    in_specs = (P(None, "row", "col"), P(None, "row", "col"), P(), P(), P(), P(), P())
    out_specs = (P(None, "row", "col"), P(None, "row", "col"), P(), P(), P(), P(), P())
    run = functools.partial(body, mesh.shape["row"], mesh.shape["col"])
    return jax.shard_map(run, mesh=mesh, in_specs=in_specs, out_specs=out_specs, check_vma=False)
```

```python
import functools
import math

import jax
import jax.numpy as jnp
import ml_dtypes
import numpy as np
from jax import lax
from jax.experimental import pallas as pl
from jax.experimental.pallas import tpu as pltpu
from jax.sharding import PartitionSpec as P

KH = 512
KW = 256

epsilon = 1e-05
threshold = 0.1
BF16 = jnp.bfloat16
F32 = jnp.float32
EVERY = ("row", "col")
VMEM_BYTES = 56 * 2**20
CHUNK_ROWS = 8
COT_EARLY = 0
OUT_LAG = 2
OUT_LATE = 2
FIRST_US = 60
TOKEN_US = 100
LAST_US = 60
MODES_US = 60
RELAYOUT_US = 12


def width_tables(width, kept):
    position = np.arange(width, dtype=np.int32)
    frequency = np.arange(kept, dtype=np.int32)
    phases = position[:, None] * frequency[None, :] % width
    angles = phases.astype(np.float32) * np.float32(2.0 * math.pi / width)
    factor = np.float32(1.0 / math.sqrt(width))
    weight = np.where(frequency == 0, 1.0, 2.0).astype(np.float32)
    cosine = np.cos(angles) * factor
    sine_values = -np.sin(angles) * factor
    plain = np.concatenate([cosine, sine_values], axis=1)
    weighted = np.concatenate([cosine * weight[None, :], sine_values * weight[None, :]], axis=1)
    return plain.astype(ml_dtypes.bfloat16), weighted.astype(ml_dtypes.bfloat16)


def height_tables(height, kept):
    position = np.arange(height, dtype=np.int32)
    indices = np.arange(kept, dtype=np.int32)
    frequency = np.where(indices < kept // 2, indices, indices + (height - kept))
    phases = position[:, None] * frequency[None, :] % height
    angles = phases.astype(np.float32) * np.float32(2.0 * math.pi / height)
    factor = np.float32(1.0 / math.sqrt(height))
    both = np.concatenate([np.cos(angles) * factor, -np.sin(angles) * factor], axis=1)
    return both.astype(ml_dtypes.bfloat16)


def dot(left, right):
    return jnp.dot(left, right, preferred_element_type=F32)


def dot_rows(left, right):
    return lax.dot_general(left, right, (((1,), (1,)), ((), ())), preferred_element_type=F32)


def dot_columns(left, right):
    return lax.dot_general(left, right, (((0,), (0,)), ((), ())), preferred_element_type=F32)


def gelu_parts(values):
    share = 0.5 * (1.0 + lax.erf(values * (1.0 / math.sqrt(2.0))))
    density = jnp.exp(-0.5 * values * values) * (1.0 / math.sqrt(2.0 * math.pi))
    return share, share + values * density


def layer_norm(field):
    centred = field - jnp.mean(field, axis=0, keepdims=True)
    variance = jnp.mean(centred * centred, axis=0, keepdims=True)
    inverse_spread = lax.rsqrt(variance + epsilon)
    return centred * inverse_spread, inverse_spread


def norm_backward(normed, inverse_spread, gradient):
    mean_grad = jnp.mean(gradient, axis=0, keepdims=True)
    mean_cross = jnp.mean(gradient * normed, axis=0, keepdims=True)
    return inverse_spread * (gradient - mean_grad - normed * mean_cross)


def modes_first(spectrum):
    parts = jnp.concatenate([spectrum[:, :KW], spectrum[:, KW:]], axis=0)
    return parts.T.astype(BF16)


def channels_first(modes):
    turned = modes.astype(F32).T.astype(BF16)
    half = turned.shape[0] // 2
    return jnp.concatenate([turned[:half], turned[half:]], axis=1)


def first_kernel(count, order, *refs):
    fields, table, out = refs[:count], refs[count], refs[count + 1]
    total = None
    for slot in range(count):
        normed, _ = layer_norm(fields[slot][0].astype(F32))
        part = dot(normed.astype(BF16), table[order[slot]])
        total = part if total is None else total + part
    out[0] = modes_first(total)


def token_kernel(count, order, *refs):
    fields, cotangents = refs[:count], refs[count : 2 * count]
    back, inverse, forward, into, into_turned, onto, onto_turned = refs[2 * count : 2 * count + 7]
    outs = refs[2 * count + 7 : 3 * count + 7]
    kept_sum, spectrum, grad_onto, grad_into = refs[3 * count + 7 :]

    @pl.when(pl.program_id(0) == 0)
    def _():
        grad_onto[...] = jnp.zeros_like(grad_onto)
        grad_into[...] = jnp.zeros_like(grad_into)

    modes = channels_first(back[0])
    total = None
    for slot in range(count):
        field = fields[slot][0].astype(F32)
        normed_in = layer_norm(field)[0].astype(BF16)
        filtered = dot(modes, inverse[order[slot]]).astype(BF16)
        summed = field + normed_in.astype(F32) + filtered.astype(F32)
        normed, inverse_spread = layer_norm(summed)
        normed_low = normed.astype(BF16)
        cotangent = cotangents[slot][0]
        before = dot(into_turned[...], normed_low)
        back_hidden = dot(onto[...], cotangent)
        share, slope = gelu_parts(before)
        hidden = (before * share).astype(BF16)
        back_before = (back_hidden * slope).astype(BF16)
        outs[slot][0] = (summed + dot(onto_turned[...], hidden)).astype(BF16)
        grad_onto[...] += dot_rows(hidden, cotangent)
        grad_into[...] += dot_rows(back_before, normed_low)
        back_normed = dot(into[...], back_before)
        grad_sum = cotangent.astype(F32) + norm_backward(normed, inverse_spread, back_normed)
        kept_sum[0, slot] = grad_sum
        part = dot(grad_sum.astype(BF16), forward[order[slot]])
        total = part if total is None else total + part
    spectrum[0] = modes_first(total)


def last_kernel(count, order, *refs):
    fields, kept_sum, back, inverse = refs[:count], refs[count], refs[count + 1], refs[count + 2]
    outs = refs[count + 3 :]
    modes = channels_first(back[0])
    for slot in range(count):
        normed, inverse_spread = layer_norm(fields[slot][0].astype(F32))
        filtered = dot(modes, inverse[order[slot]]).astype(BF16)
        grad_sum = kept_sum[0, slot]
        grad_normed = grad_sum + filtered.astype(F32)
        outs[slot][0] = (grad_sum + norm_backward(normed, inverse_spread, grad_normed)).astype(BF16)


def swap_parts(values):
    lane = lax.broadcasted_iota(jnp.int32, values.shape, 1)
    half = values.shape[1] // 2
    turned = pltpu.roll(values, half, 1)
    return jnp.where(lane < half, -turned, turned)


def to_kept(pieces, table):
    rows = jnp.concatenate([piece[0] for piece in pieces], axis=0) if len(pieces) > 1 else pieces[0][0]
    both = dot(table[...], rows)
    return both[:KH] + swap_parts(both[KH:])


def from_kept(modes, table, outs):
    both = jnp.concatenate([modes.astype(BF16), (-swap_parts(modes)).astype(BF16)], axis=0)
    rows = dot(table[...], both).astype(BF16)
    size = rows.shape[0] // len(outs)
    for at, out in enumerate(outs):
        out[0] = rows[at * size : (at + 1) * size]


def modes_kernel(count, *refs):
    pieces = refs[:count]
    forward, inverse, weight_in, bias, weight_out = refs[count : count + 5]
    outs = refs[count + 5 : 2 * count + 5]
    kept_out, hidden_out, slope_out, shrink_out = refs[2 * count + 5 :]
    kept_low = to_kept(pieces, forward).astype(BF16)
    kept_out[0] = kept_low
    before = dot(kept_low, weight_in[...]) + bias[...]
    share, slope = gelu_parts(before)
    hidden = (before * share).astype(BF16)
    hidden_out[0] = hidden
    slope_out[0] = slope
    second = dot(hidden, weight_out[...])
    level = jnp.tanh(second * (1.0 / threshold))
    shrink_out[0] = level * level
    shrunk = second - threshold * level
    from_kept(shrunk, inverse, outs)


def modes_back_kernel(count, *refs):
    pieces = refs[:count]
    kept, hidden, slope, shrink = refs[count : count + 4]
    forward, inverse, weight_in, weight_out = refs[count + 4 : count + 8]
    outs = refs[count + 8 : 2 * count + 8]
    grad_in, grad_out, grad_bias = refs[2 * count + 8 :]

    @pl.when(pl.program_id(0) == 0)
    def _():
        grad_in[...] = jnp.zeros_like(grad_in)
        grad_out[...] = jnp.zeros_like(grad_out)
        grad_bias[...] = jnp.zeros_like(grad_bias)

    grad_second = (to_kept(pieces, forward) * shrink[0]).astype(BF16)
    grad_out[...] += dot_columns(hidden[0], grad_second)
    back_spec = dot_rows(grad_second, weight_out[...])
    gate = (back_spec * slope[0]).astype(BF16)
    grad_in[...] += dot_columns(kept[0], gate)
    grad_bias[...] += jnp.sum(gate.astype(F32), axis=0, keepdims=True)
    grad_modes = dot_rows(gate, weight_in[...])
    from_kept(grad_modes, inverse, outs)


def whole(array_shape):
    return pl.BlockSpec(array_shape, lambda *at: (0,) * len(array_shape))


def by_first(array_shape):
    rest = len(array_shape) - 1
    return pl.BlockSpec((1,) + tuple(array_shape[1:]), lambda at, *_: (at,) + (0,) * rest)


def params():
    return pltpu.CompilerParams(
        dimension_semantics=("arbitrary",), vmem_limit_bytes=VMEM_BYTES
    )


def weigh(microseconds):
    return pl.CostEstimate(
        flops=int(microseconds * 1.15e9), bytes_accessed=int(microseconds * 3.6e6), transcendentals=0
    )


def leave_out(kernel, start, count):
    def run(*refs):
        kernel(*refs[:start], *refs[start + count :])

    return run


def call_rows(kernel, weight, steps, order, stepped, fixed, step_outs, fixed_outs, waited=()):
    outs = list(step_outs) + list(fixed_outs)
    return pl.pallas_call(
        leave_out(kernel, 1 + len(stepped) + len(fixed), len(waited)),
        grid_spec=pltpu.PrefetchScalarGridSpec(
            num_scalar_prefetch=1,
            grid=(steps,),
            in_specs=[by_first(a.shape) for a in stepped]
            + [whole(a.shape) for a in fixed]
            + [pl.BlockSpec(memory_space=pl.ANY)] * len(waited),
            out_specs=[by_first(a.shape) for a in step_outs] + [whole(a.shape) for a in fixed_outs],
        ),
        out_shape=outs,
        compiler_params=params(),
        cost_estimate=weigh(weight),
    )(order, *stepped, *fixed, *waited)


def call_modes(kernel, weight, steps, stepped, fixed, step_outs, fixed_outs, waited=()):
    outs = list(step_outs) + list(fixed_outs)
    return pl.pallas_call(
        leave_out(kernel, len(stepped) + len(fixed), len(waited)),
        grid=(steps,),
        in_specs=[by_first(a.shape) for a in stepped]
        + [whole(a.shape) for a in fixed]
        + [pl.BlockSpec(memory_space=pl.ANY)] * len(waited),
        out_specs=[by_first(a.shape) for a in step_outs] + [whole(a.shape) for a in fixed_outs],
        out_shape=outs,
        compiler_params=params(),
        cost_estimate=weigh(weight),
    )(*stepped, *fixed, *waited)


def split_kernel(order, field, *outs):
    rows = jnp.swapaxes(field[:, 0], 0, 1)
    size = rows.shape[0] // len(outs)
    for at, out in enumerate(outs):
        out[0] = rows[at * size : (at + 1) * size]


def split_rows(field, order, own_rows, first, chunk, count):
    channels, local_rows, local_cols = field.shape
    groups, size = local_rows // own_rows, count * chunk
    return pl.pallas_call(
        split_kernel,
        grid_spec=pltpu.PrefetchScalarGridSpec(
            num_scalar_prefetch=1,
            grid=(groups,),
            in_specs=[
                pl.BlockSpec(
                    (channels, 1, size, local_cols), lambda at, order: (0, order[at], first // size, 0)
                )
            ],
            out_specs=[
                pl.BlockSpec((1, chunk, channels, local_cols), lambda at, order: (at, 0, 0, 0))
            ]
            * count,
        ),
        out_shape=[jax.ShapeDtypeStruct((groups, chunk, channels, local_cols), BF16)] * count,
        compiler_params=params(),
        cost_estimate=weigh(RELAYOUT_US),
    )(order, field.reshape(channels, groups, own_rows, local_cols))


def join_kernel(groups, count, order, *refs):
    pieces, out = refs[: groups * count], refs[-1]
    for slot in range(groups):

        @pl.when(pl.program_id(0) == slot)
        def _():
            rows = [pieces[at * groups + slot][...] for at in range(count)]
            out[...] = jnp.swapaxes(jnp.concatenate(rows, axis=0), 0, 1)


def join_rows(total, order, own_rows, first, per_chunk):
    groups, count = len(per_chunk[0]), len(per_chunk)
    chunk, channels, local_cols = per_chunk[0][0].shape
    size = count * chunk
    pieces = [piece for chunk_pieces in per_chunk for piece in chunk_pieces]
    given = [] if total is None else [total]
    return pl.pallas_call(
        functools.partial(join_kernel, groups, count),
        grid_spec=pltpu.PrefetchScalarGridSpec(
            num_scalar_prefetch=1,
            grid=(groups,),
            in_specs=[pl.BlockSpec(piece.shape, lambda at, order: (0, 0, 0)) for piece in pieces]
            + [pl.BlockSpec(memory_space=pl.ANY)] * len(given),
            out_specs=pl.BlockSpec(
                (channels, size, local_cols),
                lambda at, order: (0, order[at] * (own_rows // size) + first // size, 0),
            ),
        ),
        out_shape=jax.ShapeDtypeStruct((channels, groups * own_rows, local_cols), BF16),
        input_output_aliases={1 + len(pieces): 0} if given else {},
        compiler_params=params(),
        cost_estimate=weigh(RELAYOUT_US),
    )(order, *pieces, *given)


def scale_kernel(factor, *refs):
    count = len(refs) // 2
    for source, out in zip(refs[:count], refs[count:]):
        out[...] = source[...] * factor


def scale(arrays, factor, waited):
    return pl.pallas_call(
        leave_out(functools.partial(scale_kernel, factor), len(arrays), len(waited)),
        in_specs=[pl.BlockSpec(memory_space=pltpu.VMEM)] * len(arrays)
        + [pl.BlockSpec(memory_space=pl.ANY)] * len(waited),
        out_specs=[pl.BlockSpec(memory_space=pltpu.VMEM)] * len(arrays),
        out_shape=[jax.ShapeDtypeStruct(a.shape, a.dtype) for a in arrays],
        compiler_params=pltpu.CompilerParams(vmem_limit_bytes=VMEM_BYTES),
    )(*arrays, *waited)


def complex_matrix(weight):
    blocks, size = weight.shape[1], weight.shape[2]

    def diagonal(part):
        rows = []
        for at in range(blocks):
            rows.append(jnp.pad(part[at], ((0, 0), (at * size, (blocks - 1 - at) * size))))
        return jnp.concatenate(rows, axis=0)

    real, imaginary = diagonal(weight[0]), diagonal(weight[1])
    return jnp.concatenate(
        [
            jnp.concatenate([real, imaginary], axis=1),
            jnp.concatenate([-imaginary, real], axis=1),
        ],
        axis=0,
    )


def complex_gradient(total, blocks):
    half = total.shape[0] // 2
    size = half // blocks
    real = total[:half, :half] + total[half:, half:]
    imaginary = total[:half, half:] - total[half:, :half]

    def blocked(part):
        return jnp.stack(
            [
                part[at * size : (at + 1) * size, at * size : (at + 1) * size]
                for at in range(blocks)
            ]
        )

    return jnp.stack([blocked(real), blocked(imaginary)])


def body(
    row_count,
    col_count,
    weather,
    cotangent,
    spectral_in,
    spectral_bias,
    spectral_out,
    project_in,
    project_out,
):
    channels, local_rows, local_cols = weather.shape
    height, width = local_rows * row_count, local_cols * col_count
    devices = row_count * col_count
    own_rows = local_rows // col_count
    chunk = min(CHUNK_ROWS, own_rows)
    chunks = own_rows // chunk
    own_modes = KW // devices
    doubled = 2 * channels
    hidden_units = project_in.shape[1]
    blocks = spectral_in.shape[1]

    paired = col_count & (col_count - 1) == 0
    column = lax.axis_index("col")
    slots = jnp.arange(col_count, dtype=jnp.int32)
    target = column ^ slots if paired else (column + slots) % col_count
    origin = column ^ slots if paired else (column - slots) % col_count

    def partner(at, slot):
        return at ^ slot if paired else (at + slot) % col_count

    def send(piece, slot):
        if slot == 0:
            return piece
        return lax.ppermute(piece, "col", [(at, partner(at, slot)) for at in range(col_count)])

    def send_back(piece, slot):
        if slot == 0:
            return piece
        return lax.ppermute(piece, "col", [(partner(at, slot), at) for at in range(col_count)])

    def exchange(spectrum):
        return lax.all_to_all(spectrum, EVERY, split_axis=0, concat_axis=0, tiled=True)

    plain, weighted = width_tables(width, KW)
    forward_plain = jnp.asarray(plain.reshape(col_count, local_cols, 2 * KW))
    forward_weighted = jnp.asarray(weighted.reshape(col_count, local_cols, 2 * KW))
    inverse_plain = jnp.asarray(
        np.ascontiguousarray(plain.reshape(col_count, local_cols, 2 * KW).transpose(0, 2, 1))
    )
    inverse_weighted = jnp.asarray(
        np.ascontiguousarray(weighted.reshape(col_count, local_cols, 2 * KW).transpose(0, 2, 1))
    )
    row_order = np.arange(height).reshape(devices, chunks, chunk).transpose(1, 0, 2).reshape(-1)
    by_rows = height_tables(height, KH)[row_order]
    modes_inverse = jnp.asarray(by_rows)
    modes_forward = jnp.asarray(np.ascontiguousarray(by_rows.T))

    matrix_in, matrix_out = complex_matrix(spectral_in), complex_matrix(spectral_out)
    bias_row = spectral_bias.reshape(1, doubled)
    into_turned, onto_turned = project_in.T, project_out.T

    pair = 2 if chunks % 2 == 0 else 1

    def field_pieces(field, at):
        split = split_rows(field, target, own_rows, at * chunk, chunk, pair)
        return [[rows[slot] for slot in range(col_count)] for rows in split]

    def send_all(pieces):
        return [send(piece, slot) for slot, piece in enumerate(pieces)]

    def to_modes(spectrum):
        parted = spectrum.reshape(chunk, devices, own_modes, doubled).transpose(1, 0, 2, 3)
        got = exchange(parted.reshape(devices, chunk * own_modes, doubled))
        got = got.reshape(devices * chunk, own_modes, doubled)
        return got.transpose(1, 0, 2)

    def to_rows(modes):
        parted = modes.reshape(own_modes, devices, chunk, doubled).transpose(1, 2, 0, 3)
        got = exchange(parted.reshape(devices, chunk * own_modes, doubled))
        got = got.reshape(devices, chunk, own_modes, doubled).transpose(1, 0, 2, 3)
        return got.reshape(chunk, KW, doubled)

    def place(total, pieces, at):
        for slot in range(col_count):
            total = lax.dynamic_update_slice(
                total, pieces[slot].transpose(1, 0, 2), (0, target[slot] * own_rows + at * chunk, 0)
            )
        return total

    def shape(*dims, kind=BF16):
        return jax.ShapeDtypeStruct(dims, kind)

    piece_shape = shape(chunk, channels, local_cols)
    spectrum_shape = shape(chunk, KW, doubled)
    rows_shape = shape(own_modes, devices * chunk, doubled)

    starts = range(0, chunks, pair)
    weather_now = [send_all(x) for at in starts for x in field_pieces(weather, at)]
    cot_parts = [x for at in starts for x in field_pieces(cotangent, at)]
    cot_now = [send_all(x) for x in cot_parts]
    spectra = []
    for at in range(chunks):
        (spectrum,) = call_rows(
            functools.partial(first_kernel, col_count),
            FIRST_US,
            chunk,
            origin,
            weather_now[at],
            [forward_plain],
            [spectrum_shape],
            [],
            waited=[cot_parts[0][0], cot_parts[-1][0]] if at == chunks - 1 else [],
        )
        spectra.append(to_modes(spectrum))

    mode_dims = (own_modes, KH, doubled)
    results = call_modes(
        functools.partial(modes_kernel, chunks),
            MODES_US,
        own_modes,
        spectra,
        [modes_forward, modes_inverse, matrix_in, bias_row, matrix_out],
        [rows_shape] * chunks
        + [shape(*mode_dims), shape(*mode_dims), shape(*mode_dims, kind=F32), shape(*mode_dims, kind=F32)],
        [],
        waited=[piece for pieces in cot_now[:COT_EARLY] for piece in pieces],
    )
    back, saved = results[:chunks], results[chunks:]

    outputs, kept_sums, grad_spectra, grad_onto, grad_into = [], [], [], 0.0, 0.0
    for at in range(chunks):
        results = call_rows(
            functools.partial(token_kernel, col_count),
            TOKEN_US,
            chunk,
            origin,
            weather_now[at] + cot_now[at] + [to_rows(back[at])],
            [
                inverse_weighted,
                forward_weighted,
                project_in,
                into_turned,
                project_out,
                onto_turned,
            ],
            [piece_shape] * col_count
            + [shape(chunk, col_count, channels, local_cols, kind=F32), spectrum_shape],
            [shape(hidden_units, channels, kind=F32)] * 2,
            waited=outputs[at - OUT_LAG] if at >= OUT_LAG else [],
        )
        spectrum = results[col_count + 1]
        outputs.append([send_back(results[slot], slot) for slot in range(col_count)])
        kept_sums.append(results[col_count])
        grad_spectra.append(to_modes(spectrum))
        grad_onto = grad_onto + results[col_count + 2]
        grad_into = grad_into + results[col_count + 3]
    early = max(chunks - OUT_LATE, 0)
    results = call_modes(
        functools.partial(modes_back_kernel, chunks),
            MODES_US,
        own_modes,
        grad_spectra + list(saved),
        [modes_forward, modes_inverse, matrix_in, matrix_out],
        [rows_shape] * chunks,
        [
            shape(doubled, doubled, kind=F32),
            shape(doubled, doubled, kind=F32),
            shape(1, doubled, kind=F32),
        ],
        waited=[piece for pieces in outputs[:early] for piece in pieces],
    )
    grad_back = results[:chunks]
    grad_in_total, grad_out_total, grad_bias_total = results[chunks:]

    spectral_grads = jnp.stack(
        [complex_gradient(grad_in_total, blocks), complex_gradient(grad_out_total, blocks)]
    )
    packed = jnp.concatenate([spectral_grads.reshape(-1), grad_bias_total.reshape(-1)])
    token_grads, packed = lax.psum(
        (jnp.concatenate([grad_onto, grad_into], axis=0), packed.reshape(-1, 128)), EVERY
    )

    grads = []
    for at in range(chunks):
        results = call_rows(
            functools.partial(last_kernel, col_count),
            LAST_US,
            chunk,
            origin,
            weather_now[at] + [kept_sums[at], to_rows(grad_back[at])],
            [inverse_plain],
            [piece_shape] * col_count,
            [],
            waited=outputs[early + at] if early + at < chunks else [],
        )
        grads.append([send_back(results[slot], slot) for slot in range(col_count)])
    token_grads, packed = scale(
        [token_grads, packed], 1.0 / height, grads[max(chunks - 2, 0)]
    )

    layer_out = None
    for at in range(0, chunks, pair):
        layer_out = join_rows(layer_out, target, own_rows, at * chunk, outputs[at : at + pair])
    grad_weather = join_rows(None, target, own_rows, 0, grads[:pair])
    for at in range(pair, chunks):
        grad_weather = place(grad_weather, grads[at], at)
    packed = packed.reshape(-1)
    spectral_grads = packed[:-doubled].reshape(spectral_grads.shape)
    return (
        layer_out,
        grad_weather,
        token_grads[hidden_units:].T,
        token_grads[:hidden_units],
        spectral_grads[0],
        spectral_grads[1],
        packed[-doubled:].reshape(spectral_bias.shape),
    )


def solution(mesh):
    in_specs = (P(None, "row", "col"), P(None, "row", "col"), P(), P(), P(), P(), P())
    out_specs = (P(None, "row", "col"), P(None, "row", "col"), P(), P(), P(), P(), P())
    run = functools.partial(body, mesh.shape["row"], mesh.shape["col"])
    return jax.shard_map(run, mesh=mesh, in_specs=in_specs, out_specs=out_specs, check_vma=False)
```
